32 devices in a mesh: group: 4 (over y, x), member: 8 (over z, core).
Axes of the slice: x: 2, y: 2, z: 4, core: 2. Of those that a mesh axis runs over, the one named last changes fastest.
Arguments:
- level_set: bfloat16 [256, 128, 2048], P(('group', 'member')), may hold values from -6 to 6
- ray_length: int32 [128, 2048], replicated, may hold values from 64 to 256
- member_flip: int32 [4], P('group'), may hold values from 0 to 7
- group_flip: int32 [1], replicated, may hold values from 0 to 31
Outputs:
- final_image: float32 [5, 262144], P(None, ('group', 'member'))
The draws below stay inside these ranges and needn't reach their ends.
Inputs may be any that keep to these rules, and one draw needn't show every extreme that they name: `ray_length`: each entry is a ray's length in depth samples. `member_flip`: bit patterns of the viewing direction along the splits inside a block. `group_flip`: bit pattern of the viewing direction along all splits.
All inputs are finite; a program needn't handle non-finite values.
Results may differ from the reference program's by a relative error of at most 0.0003.
Values sent between devices are 32-bit elements; how exact they have to be, the bound alone decides.
A program may use at most 128 MiB of HBM per device.

```python
import math
import jax
import jax.numpy as jnp
from jax import lax

ROWS = 128
COLS = 2048
DEPTH_DEV = 8
DEPTHS = 256
N_GROUP = 4
N_MEMBER = 8


def plant(result, rng, low, high):
    longest = result.shape.index(max(result.shape))
    spots = []
    for shift in (0, 1):
        where = [jax.random.randint(jax.random.fold_in(rng, axis), (), 0, length) for axis, length in enumerate(result.shape)]
        where[longest] = (where[longest] + shift) % result.shape[longest]
        spots.append(tuple(where))
    return result.at[spots[0]].set(low).at[spots[1]].set(high)


def level_of(own_key, extent, split, smallest, largest):
    gain = 1.0
    for position, parts in split:
        heights = jax.random.uniform(jax.random.fold_in(jax.random.fold_in(own_key, 6), position), (parts,), jnp.float32, smallest / len(split), largest / len(split))
        gain = gain * jnp.repeat(jnp.exp(heights), extent[position] // parts).reshape((-1,) + (1,) * (len(extent) - 1 - position))
    return gain


def scatter_about(rng, shape, spread, limit, shards=(), kind=jnp.bfloat16):
    gain = level_of(rng, shape, shards, -0.22, 0.18) if shards else 1.0
    drawn = jax.random.normal(rng, shape, jnp.float32) * spread * gain
    return jnp.minimum(jnp.maximum(drawn, -limit), limit).astype(kind)


def setup_inputs(seed: int = 0) -> dict:
    keys = jax.random.split(jax.random.key(seed), 5)
    return {
        "level_set": scatter_about(keys[0], (DEPTHS, ROWS, COLS), 1.0, 6.0, ((0, 32),)),
        "ray_length": plant(jax.random.randint(keys[1], (ROWS, COLS), DEPTHS // 4, DEPTHS + 1), jax.random.fold_in(keys[1], 1), DEPTHS // 4, DEPTHS).astype(jnp.int32),
        "member_flip": plant(jax.random.randint(keys[2], (N_GROUP,), 0, N_MEMBER), jax.random.fold_in(keys[2], 1), 0, N_MEMBER - 1).astype(jnp.int32),
        "group_flip": jax.random.randint(keys[3], (1,), 0, N_GROUP * N_MEMBER).astype(jnp.int32),
    }


def march_slab(slab_values, first_sample, ray_length, depths, member_count):
    slices = slab_values.shape[0]
    level_values = slab_values.astype(jnp.float32)
    padded = jnp.pad(level_values, ((0, 0), (1, 1), (1, 1)), mode='edge')
    across = (padded[:, 1:-1, 2:] - padded[:, 1:-1, :-2]) * 0.5
    downward = (padded[:, 2:, 1:-1] - padded[:, :-2, 1:-1]) * 0.5
    facing = (0.48 * across + 0.6 * downward + 0.64) * lax.rsqrt(across * across + downward * downward + 1.0)
    shading = 0.25 + 0.75 * jnp.maximum(facing, 0.0)
    sample = first_sample.astype(jnp.int32) + jnp.arange(slices, dtype=jnp.int32)
    active_mask = sample[:, None, None] < ray_length[None, :, :]
    opacity = jnp.where(active_mask, 9.0 / depths * jnp.exp(-4.0 * level_values * level_values), jnp.float32(0.0))
    through = jnp.cumprod(1.0 - opacity, axis=0)
    before = jnp.concatenate([jnp.ones_like(through[:1]), through[:-1]], axis=0)
    weight = before * opacity
    sample_real = sample.astype(jnp.float32)
    phase_angle = 2.0 * math.pi / (slices * member_count) * sample_real
    channel_shift = 2.0 * math.pi / 3.0 * jnp.arange(3, dtype=jnp.float32)
    banding = 0.5 + 0.5 * jnp.cos(phase_angle[None, :] + channel_shift[:, None])
    colors = jnp.tensordot(banding, weight * shading, axes=1, precision=lax.Precision.HIGHEST)
    distance = jnp.tensordot((sample_real + 0.5) / depths, weight, axes=1, precision=lax.Precision.HIGHEST)
    return jnp.concatenate([colors, distance[None], (1.0 - through[-1])[None]], axis=0)

def reference(level_set, ray_length, member_flip, group_flip):
    whole_flip = group_flip[0].astype(jnp.int32)
    high_flip = whole_flip // N_MEMBER
    low_flip = whole_flip % N_MEMBER

    def visit_slab(step_index, carry):
        shaded, transmit = carry
        depth_rank = jnp.asarray(step_index).astype(jnp.int32)
        group_rank = depth_rank // N_MEMBER
        member_rank = depth_rank % N_MEMBER
        group_id = jnp.bitwise_xor(group_rank, high_flip)
        member_id = jnp.bitwise_xor(jnp.bitwise_xor(member_rank, low_flip), member_flip[group_id])
        start_row = ((group_id * N_MEMBER + member_id) * DEPTH_DEV).astype(jnp.int32)
        slab_values = lax.dynamic_slice_in_dim(level_set, start_row, DEPTH_DEV, 0)
        partial_value = march_slab(slab_values, depth_rank * DEPTH_DEV, ray_length, DEPTHS, N_MEMBER)
        shaded = shaded + transmit[None] * partial_value[:4]
        transmit = transmit * (1.0 - partial_value[4])
        return (shaded, transmit)
    start_state = (jnp.zeros((4, ROWS, COLS), jnp.float32), jnp.ones((ROWS, COLS), jnp.float32))
    shaded, transmit = lax.fori_loop(0, N_GROUP * N_MEMBER, visit_slab, start_state)
    final_image = jnp.concatenate([shaded, (1.0 - transmit)[None]], axis=0)
    return final_image.reshape(5, ROWS * COLS)
```

```python
import functools
import math

import jax
import jax.numpy as jnp
from jax import lax
from jax.experimental import pallas as pl
from jax.experimental.pallas import tpu as pltpu
from jax.sharding import PartitionSpec as P

MESH = pl.DeviceIdType.MESH
LANES = 128
PAD = 8


def flip_bit(index, bit):
    own = (index // (1 << bit)) % 2
    return index + (1 - 2 * own) * (1 << bit), own


def kernel(cfg, level_ref, ray_ref, mflip_ref, gflip_ref, out_ref,
           lev, part, *rest):
    groups, members, bits, slices, rows, cols, subs, block = cfg
    depths = slices * members * groups
    arrive, from_group = rest[:bits], rest[bits]
    send_sem, recv_sem, gsend_sem, grecv_sem = rest[bits + 1:]
    chunks = groups * subs
    chunk_rows = rows // groups
    chunk_cols = cols // subs
    tiles_wide = chunk_cols // LANES
    width = min(512, chunk_cols)

    group_id = lax.axis_index("group")
    member_id = lax.axis_index("member")
    whole_flip = gflip_ref[0]
    member_mask = jnp.bitwise_xor(mflip_ref[0], whole_flip % members)
    group_mask = whole_flip // members
    member_rank = jnp.bitwise_xor(member_id, member_mask)
    group_rank = jnp.bitwise_xor(group_id, group_mask)
    first = (group_rank * members + member_rank) * slices

    barrier = pltpu.get_barrier_semaphore()
    for bit in range(bits):
        partner, _ = flip_bit(member_id, bit)
        pl.semaphore_signal(barrier, inc=1, device_id=(group_id, partner), device_id_type=MESH)
    for step in range(groups - 1):
        other = (group_id + 1 + step) % groups
        pl.semaphore_signal(barrier, inc=1, device_id=(other, member_id), device_id_type=MESH)

    for k in range(slices):
        @pl.loop(0, rows // 16)
        def _(i):
            r = pl.multiple_of(i * 16, 16)
            value = level_ref[k, pl.ds(r, 16), :].astype(jnp.float32)
            at = pl.ds(pl.multiple_of(r + PAD, 8), 16)
            lev[k, at, LANES:LANES + cols] = value
            lev[k, at, 0:LANES] = jnp.broadcast_to(value[:, 0:1], (16, LANES))
            lev[k, at, LANES + cols:] = jnp.broadcast_to(value[:, cols - 1:cols], (16, LANES))
        lev[k, 0:PAD, :] = jnp.broadcast_to(lev[k, PAD:PAD + 1, :], (PAD, cols + 2 * LANES))
        lev[k, PAD + rows:, :] = jnp.broadcast_to(
            lev[k, PAD + rows - 1:PAD + rows, :], (PAD, cols + 2 * LANES))

    period = slices * members
    base_phase = (2.0 * math.pi / period) * (first % period).astype(jnp.float32)
    band = []
    for c in range(3):
        angle = jnp.full((8, LANES), base_phase + 2.0 * math.pi / 3.0 * c, jnp.float32)
        band.append((0.5 * jnp.cos(angle), 0.5 * jnp.sin(angle)))
    first_real = first.astype(jnp.float32)

    def march(t):
        target = (group_id + 1 + t // subs) % groups
        sub = t % subs
        flat = part.at[t].reshape(5, members * block, LANES)

        @pl.loop(0, (chunk_rows // 8) * (chunk_cols // width))
        def _(i):
            local = (i // (chunk_cols // width)) * 8
            local_col = (i % (chunk_cols // width)) * width
            r0 = pl.multiple_of(target * chunk_rows + local, 8)
            c0 = pl.multiple_of(sub * chunk_cols + local_col, LANES)
            left_samples = ray_ref[pl.ds(r0, 8), pl.ds(c0, width)] - first
            through = jnp.ones((8, width), jnp.float32)
            plain = jnp.zeros((8, width), jnp.float32)
            even = odd = distance = plain
            for k in range(slices):
                wide = lev[k, pl.ds(pl.multiple_of(r0 + PAD, 8), 8), pl.ds(c0, width + 2 * LANES)]
                total = width + 2 * LANES
                left = pltpu.roll(wide, 1, 1)[:, LANES:LANES + width]
                right = pltpu.roll(wide, total - 1, 1)[:, LANES:LANES + width]
                phi = wide[:, LANES:LANES + width]
                tall = lev[k, pl.ds(r0, 24), pl.ds(pl.multiple_of(c0 + LANES, LANES), width)]
                across = right - left
                downward = tall[9:17] - tall[7:15]
                facing = (0.48 * across + 0.6 * downward + 1.28) * lax.rsqrt(
                    across * across + downward * downward + 4.0)
                shading = 0.25 + 0.75 * jnp.maximum(facing, 0.0)
                opacity = jnp.exp2(phi * phi * (-4.0 / math.log(2.0)) + math.log2(9.0 / depths))
                opacity = jnp.where(left_samples > k, opacity, 0.0)
                weight = through * opacity
                through = through - weight
                distance = distance + weight * ((first_real + (k + 0.5)) / depths)
                shaded = weight * shading
                plain = plain + shaded
                even = even + shaded * math.cos(2.0 * math.pi * k / period)
                if k:
                    odd = odd + shaded * math.sin(2.0 * math.pi * k / period)
            for j in range(width // LANES):
                cut = slice(j * LANES, (j + 1) * LANES)
                at = pl.ds(local * tiles_wide + local_col // LANES + j, 8, stride=tiles_wide)
                for c in range(3):
                    flat[c, at, :] = (0.5 * plain[:, cut] + band[c][0] * even[:, cut]
                                      - band[c][1] * odd[:, cut])
                flat[3, at, :] = distance[:, cut]
                flat[4, at, :] = through[:, cut]

    def half(source, t, own):
        return source.at[t, :, :, own]

    def swap(bit, t):
        partner, own = flip_bit(member_id, bit)
        source = part if bit == 0 else arrive[bit - 1]
        return pltpu.make_async_remote_copy(
            src_ref=half(source, t, 1 - own), dst_ref=landing(bit, t),
            send_sem=send_sem.at[bit, t], recv_sem=recv_sem.at[bit, t],
            device_id=(group_id, partner), device_id_type=MESH)

    def landing(bit, t):
        held = arrive[bit].at[t]
        if bit < bits - 1:
            held = held.reshape(5, members >> (bit + 1), block, LANES)
        return held

    def hand_over(t):
        target = (group_id + 1 + t // subs) % groups
        return pltpu.make_async_remote_copy(
            src_ref=arrive[bits - 1].at[t], dst_ref=from_group.at[t],
            send_sem=gsend_sem.at[t], recv_sem=grecv_sem.at[t],
            device_id=(target, member_id), device_id_type=MESH)

    def blend(bit, t):
        _, own = flip_bit(member_id, bit)
        swap(bit, t).wait_recv()
        source = part if bit == 0 else arrive[bit - 1]
        mine_front = jnp.bitwise_and(jnp.right_shift(member_rank, bit), 1) == 0
        count = members >> (bit + 1)
        target = landing(bit, t)

        @pl.loop(0, count)
        def _(z):
            def kept(c):
                return source[t, c, z, own]

            def place(c):
                return (c, z) if bit < bits - 1 else (c, 0)
            mine, theirs = kept(4), target[place(4)]
            keep_scale = jnp.where(mine_front, 1.0, theirs)
            come_scale = jnp.where(mine_front, mine, 1.0)
            for c in range(4):
                target[place(c)] = keep_scale * kept(c) + come_scale * target[place(c)]
            target[place(4)] = mine * theirs

    pl.semaphore_wait(barrier, bits + groups - 1)

    delay = [0] + [2 * b for b in range(1, bits)]

    @pl.loop(0, chunks + delay[-1])
    def _(t):
        @pl.when(t < chunks)
        def _():
            march(t)
            swap(0, t).start()
        for bit in range(bits):
            now = t - delay[bit]

            @pl.when((now >= 0) & (now < chunks))
            def _():
                blend(bit, now)
                if bit < bits - 1:
                    swap(bit + 1, now).start()
                else:
                    @pl.when(now < chunks - subs)
                    def _():
                        hand_over(now).start()

    @pl.loop(0, chunks - subs)
    def _(t):
        hand_over(t).wait_recv()

    senders = [(group_id + 2 * groups - 1 - i) % groups for i in range(groups)]
    ranks = [jnp.bitwise_xor(s, group_mask) for s in senders]
    for s in range(subs):
        images = [from_group.at[i * subs + s] for i in range(groups - 1)]
        images.append(arrive[bits - 1].at[(groups - 1) * subs + s, :, 0])

        def piece(i, c):
            if i < groups - 1:
                return images[i][c, 0]
            return images[i][c]
        clear = [piece(i, 4) for i in range(groups)]
        total = [None] * 4
        for i in range(groups):
            ahead = None
            for h in range(groups):
                if h != i:
                    term = jnp.where(ranks[h] < ranks[i], clear[h], 1.0)
                    ahead = term if ahead is None else ahead * term
            for c in range(4):
                term = ahead * piece(i, c)
                total[c] = term if total[c] is None else total[c] + term
        for c in range(4):
            out_ref[c, s] = total[c]
        out_ref[4, s] = 1.0 - functools.reduce(lambda a, b: a * b, clear)

    @pl.loop(0, chunks)
    def _(t):
        for bit in range(bits):
            swap(bit, t).wait_send()

    @pl.loop(0, chunks - subs)
    def _(t):
        hand_over(t).wait_send()


def body(groups, members, level_set, ray_length, member_flip, group_flip):
    slices, rows, cols = level_set.shape
    bits = members.bit_length() - 1
    pixels = rows * cols // (groups * members)
    whole_rows = pixels % cols == 0
    subs = 2 if whole_rows and pixels % (2 * 8 * LANES) == 0 else 1
    block = pixels // LANES // subs
    chunks = groups * subs
    cfg = (groups, members, bits, slices, rows, cols, subs, block)
    arrive = []
    for bit in range(bits):
        count = members >> (bit + 1)
        shape = (count // 2, 2) if bit < bits - 1 else (1,)
        arrive.append(pltpu.VMEM((chunks, 5) + shape + (block, LANES), jnp.float32))
    vmem = pl.BlockSpec(memory_space=pltpu.VMEM)
    smem = pl.BlockSpec(memory_space=pltpu.SMEM)
    image = pl.pallas_call(
        functools.partial(kernel, cfg),
        out_shape=jax.ShapeDtypeStruct((5, subs, block, LANES), jnp.float32),
        in_specs=[vmem, vmem, smem, smem],
        out_specs=vmem,
        scratch_shapes=[
            pltpu.VMEM((slices, rows + 2 * PAD, cols + 2 * LANES), jnp.float32),
            pltpu.VMEM((chunks, 5, members // 2, 2, block, LANES), jnp.float32),
            *arrive,
            pltpu.VMEM((chunks - subs, 5, 1, block, LANES), jnp.float32),
            pltpu.SemaphoreType.DMA((bits, chunks)),
            pltpu.SemaphoreType.DMA((bits, chunks)),
            pltpu.SemaphoreType.DMA((chunks - subs,)),
            pltpu.SemaphoreType.DMA((chunks - subs,)),
        ],
        compiler_params=pltpu.CompilerParams(
            collective_id=0, has_side_effects=True, vmem_limit_bytes=48 * 1024 * 1024),
        cost_estimate=pl.CostEstimate(
            flops=40 * slices * rows * cols, bytes_accessed=level_set.size * 2,
            transcendentals=2 * slices * rows * cols),
    )(level_set, ray_length, member_flip, group_flip)
    if subs > 1:
        image = image.reshape(5, subs, pixels // cols, cols // subs).transpose(0, 2, 1, 3)
    return image.reshape(5, pixels)


def solution(mesh):
    in_specs = (P(("group", "member"), None, None), P(), P("group"), P())
    out_specs = P(None, ("group", "member"))
    run = functools.partial(body, mesh.shape["group"], mesh.shape["member"])
    return jax.shard_map(run, mesh=mesh, in_specs=in_specs, out_specs=out_specs, check_vma=False)
```

```python
import functools
import math

import jax
import jax.numpy as jnp
from jax import lax
from jax.experimental import pallas as pl
from jax.experimental.pallas import tpu as pltpu
from jax.sharding import PartitionSpec as P

MESH = pl.DeviceIdType.MESH
LANES = 128
PAD = 8


def flip_bit(index, bit):
    own = (index // (1 << bit)) % 2
    return index + (1 - 2 * own) * (1 << bit), own


def kernel(cfg, level_ref, ray_ref, mflip_ref, gflip_ref, out_ref,
           level_here, ray_here, fetch_sem, ray_sem, lev, part, *rest):
    groups, members, bits, slices, rows, cols, subs, block = cfg
    depths = slices * members * groups
    arrive, from_group = rest[:bits], rest[bits]
    send_sem, recv_sem, gsend_sem, grecv_sem = rest[bits + 1:]
    chunks = groups * subs
    chunk_rows = rows // groups
    chunk_cols = cols // subs
    tiles_wide = chunk_cols // LANES
    width = min(512, chunk_cols)

    group_id = lax.axis_index("group")
    member_id = lax.axis_index("member")
    whole_flip = gflip_ref[0]
    member_mask = jnp.bitwise_xor(mflip_ref[0], whole_flip % members)
    group_mask = whole_flip // members
    member_rank = jnp.bitwise_xor(member_id, member_mask)
    group_rank = jnp.bitwise_xor(group_id, group_mask)
    first = (group_rank * members + member_rank) * slices

    barrier = pltpu.get_barrier_semaphore()
    for bit in range(bits):
        partner, _ = flip_bit(member_id, bit)
        pl.semaphore_signal(barrier, inc=1, device_id=(group_id, partner), device_id_type=MESH)
    for step in range(groups - 1):
        other = (group_id + 1 + step) % groups
        pl.semaphore_signal(barrier, inc=1, device_id=(other, member_id), device_id_type=MESH)

    strips = rows // 16
    start_row = ((group_id + 1) % groups) * chunk_rows
    first_strip = (start_row + chunk_rows % 16) // 16 + strips - 1
    early = min(chunk_rows // 16 + 2, strips)

    def strip_row(p):
        return pl.multiple_of(((first_strip + p) % strips) * 16, 16)

    def fetch(p):
        at = pl.ds(strip_row(p), 16)
        return pltpu.make_async_copy(level_ref.at[:, at, :], level_here.at[:, at, :], fetch_sem.at[p])

    rays = pltpu.make_async_copy(ray_ref, ray_here, ray_sem)
    for p in range(early):
        fetch(p).start()
    rays.start()
    for p in range(early, strips):
        fetch(p).start()

    def unpack(p):
        fetch(p).wait()
        r = strip_row(p)
        for k in range(slices):
            value = level_here[k, pl.ds(r, 16), :].astype(jnp.float32)
            at = pl.ds(pl.multiple_of(r + PAD, 8), 16)
            lev[k, at, LANES:LANES + cols] = value
            lev[k, at, 0:LANES] = jnp.broadcast_to(value[:, 0:1], (16, LANES))
            lev[k, at, LANES + cols:] = jnp.broadcast_to(value[:, cols - 1:cols], (16, LANES))

        @pl.when(r == 0)
        def _():
            for k in range(slices):
                lev[k, 0:PAD, :] = jnp.broadcast_to(
                    lev[k, PAD:PAD + 1, :], (PAD, cols + 2 * LANES))

        @pl.when(r == rows - 16)
        def _():
            for k in range(slices):
                lev[k, PAD + rows:, :] = jnp.broadcast_to(
                    lev[k, PAD + rows - 1:PAD + rows, :], (PAD, cols + 2 * LANES))

    period = slices * members
    base_phase = (2.0 * math.pi / period) * (first % period).astype(jnp.float32)
    band = []
    for c in range(3):
        angle = jnp.full((8, LANES), base_phase + 2.0 * math.pi / 3.0 * c, jnp.float32)
        band.append((0.5 * jnp.cos(angle), 0.5 * jnp.sin(angle)))
    first_real = first.astype(jnp.float32)

    def march(t):
        target = (group_id + 1 + t // subs) % groups
        sub = t % subs
        flat = part.at[t].reshape(5, members * block, LANES)

        @pl.loop(0, (chunk_rows // 8) * (chunk_cols // width))
        def _(i):
            local = (i // (chunk_cols // width)) * 8
            local_col = (i % (chunk_cols // width)) * width
            r0 = pl.multiple_of(target * chunk_rows + local, 8)
            c0 = pl.multiple_of(sub * chunk_cols + local_col, LANES)
            left_samples = ray_here[pl.ds(r0, 8), pl.ds(c0, width)] - first
            through = jnp.ones((8, width), jnp.float32)
            plain = jnp.zeros((8, width), jnp.float32)
            even = odd = distance = plain
            for k in range(slices):
                wide = lev[k, pl.ds(pl.multiple_of(r0 + PAD, 8), 8), pl.ds(c0, width + 2 * LANES)]
                total = width + 2 * LANES
                left = pltpu.roll(wide, 1, 1)[:, LANES:LANES + width]
                right = pltpu.roll(wide, total - 1, 1)[:, LANES:LANES + width]
                phi = wide[:, LANES:LANES + width]
                tall = lev[k, pl.ds(r0, 24), pl.ds(pl.multiple_of(c0 + LANES, LANES), width)]
                across = right - left
                downward = tall[9:17] - tall[7:15]
                facing = (0.48 * across + 0.6 * downward + 1.28) * lax.rsqrt(
                    across * across + downward * downward + 4.0)
                shading = 0.25 + 0.75 * jnp.maximum(facing, 0.0)
                opacity = jnp.exp2(phi * phi * (-4.0 / math.log(2.0)) + math.log2(9.0 / depths))
                opacity = jnp.where(left_samples > k, opacity, 0.0)
                weight = through * opacity
                through = through - weight
                distance = distance + weight * ((first_real + (k + 0.5)) / depths)
                shaded = weight * shading
                plain = plain + shaded
                even = even + shaded * math.cos(2.0 * math.pi * k / period)
                if k:
                    odd = odd + shaded * math.sin(2.0 * math.pi * k / period)
            for j in range(width // LANES):
                cut = slice(j * LANES, (j + 1) * LANES)
                at = pl.ds(local * tiles_wide + local_col // LANES + j, 8, stride=tiles_wide)
                for c in range(3):
                    flat[c, at, :] = (0.5 * plain[:, cut] + band[c][0] * even[:, cut]
                                      - band[c][1] * odd[:, cut])
                flat[3, at, :] = distance[:, cut]
                flat[4, at, :] = through[:, cut]

    def half(source, t, own):
        return source.at[t, :, :, own]

    def swap(bit, t):
        partner, own = flip_bit(member_id, bit)
        source = part if bit == 0 else arrive[bit - 1]
        return pltpu.make_async_remote_copy(
            src_ref=half(source, t, 1 - own), dst_ref=landing(bit, t),
            send_sem=send_sem.at[bit, t], recv_sem=recv_sem.at[bit, t],
            device_id=(group_id, partner), device_id_type=MESH)

    def landing(bit, t):
        held = arrive[bit].at[t]
        if bit < bits - 1:
            held = held.reshape(5, members >> (bit + 1), block, LANES)
        return held

    def hand_over(t):
        target = (group_id + 1 + t // subs) % groups
        return pltpu.make_async_remote_copy(
            src_ref=arrive[bits - 1].at[t], dst_ref=from_group.at[t],
            send_sem=gsend_sem.at[t], recv_sem=grecv_sem.at[t],
            device_id=(target, member_id), device_id_type=MESH)

    def blend(bit, t):
        _, own = flip_bit(member_id, bit)
        swap(bit, t).wait_recv()
        source = part if bit == 0 else arrive[bit - 1]
        mine_front = jnp.bitwise_and(jnp.right_shift(member_rank, bit), 1) == 0
        count = members >> (bit + 1)
        target = landing(bit, t)

        @pl.loop(0, count)
        def _(z):
            def kept(c):
                return source[t, c, z, own]

            def place(c):
                return (c, z) if bit < bits - 1 else (c, 0)
            mine, theirs = kept(4), target[place(4)]
            keep_scale = jnp.where(mine_front, 1.0, theirs)
            come_scale = jnp.where(mine_front, mine, 1.0)
            for c in range(4):
                target[place(c)] = keep_scale * kept(c) + come_scale * target[place(c)]
            target[place(4)] = mine * theirs

    pl.loop(0, early)(unpack)
    rays.wait()
    march(0)
    pl.semaphore_wait(barrier, bits + groups - 1)

    delay = [0] + [3 * b - 1 for b in range(1, bits)]

    @pl.loop(0, chunks + delay[-1])
    def _(t):
        @pl.when(t < chunks)
        def _():
            swap(0, t).start()

        @pl.when(t == subs - 1)
        def _():
            pl.loop(early, strips)(unpack)

        @pl.when(t < chunks - 1)
        def _():
            march(t + 1)
        for bit in range(bits):
            now = t - delay[bit]

            @pl.when((now >= 0) & (now < chunks))
            def _():
                blend(bit, now)
                if bit < bits - 1:
                    swap(bit + 1, now).start()
                else:
                    @pl.when(now < chunks - subs)
                    def _():
                        hand_over(now).start()

    @pl.loop(0, chunks - subs)
    def _(t):
        hand_over(t).wait_recv()

    senders = [(group_id + 2 * groups - 1 - i) % groups for i in range(groups)]
    ranks = [jnp.bitwise_xor(s, group_mask) for s in senders]
    for s in range(subs):
        images = [from_group.at[i * subs + s] for i in range(groups - 1)]
        images.append(arrive[bits - 1].at[(groups - 1) * subs + s, :, 0])

        def piece(i, c):
            if i < groups - 1:
                return images[i][c, 0]
            return images[i][c]
        clear = [piece(i, 4) for i in range(groups)]
        total = [None] * 4
        for i in range(groups):
            ahead = None
            for h in range(groups):
                if h != i:
                    term = jnp.where(ranks[h] < ranks[i], clear[h], 1.0)
                    ahead = term if ahead is None else ahead * term
            for c in range(4):
                term = ahead * piece(i, c)
                total[c] = term if total[c] is None else total[c] + term
        for c in range(4):
            out_ref[c, s] = total[c]
        out_ref[4, s] = 1.0 - functools.reduce(lambda a, b: a * b, clear)

    @pl.loop(0, chunks)
    def _(t):
        for bit in range(bits):
            swap(bit, t).wait_send()

    @pl.loop(0, chunks - subs)
    def _(t):
        hand_over(t).wait_send()


def body(groups, members, level_set, ray_length, member_flip, group_flip):
    slices, rows, cols = level_set.shape
    bits = members.bit_length() - 1
    pixels = rows * cols // (groups * members)
    whole_rows = pixels % cols == 0
    subs = 1
    while whole_rows and subs < 4 and pixels % (2 * subs * 8 * LANES) == 0:
        subs *= 2
    block = pixels // LANES // subs
    chunks = groups * subs
    cfg = (groups, members, bits, slices, rows, cols, subs, block)
    arrive = []
    for bit in range(bits):
        count = members >> (bit + 1)
        shape = (count // 2, 2) if bit < bits - 1 else (1,)
        arrive.append(pltpu.VMEM((chunks, 5) + shape + (block, LANES), jnp.float32))
    vmem = pl.BlockSpec(memory_space=pltpu.VMEM)
    anywhere = pl.BlockSpec(memory_space=pl.ANY)
    smem = pl.BlockSpec(memory_space=pltpu.SMEM)
    image = pl.pallas_call(
        functools.partial(kernel, cfg),
        out_shape=jax.ShapeDtypeStruct((5, subs, block, LANES), jnp.float32),
        in_specs=[anywhere, anywhere, smem, smem],
        out_specs=vmem,
        scratch_shapes=[
            pltpu.VMEM((slices, rows, cols), level_set.dtype),
            pltpu.VMEM((rows, cols), ray_length.dtype),
            pltpu.SemaphoreType.DMA((rows // 16,)),
            pltpu.SemaphoreType.DMA,
            pltpu.VMEM((slices, rows + 2 * PAD, cols + 2 * LANES), jnp.float32),
            pltpu.VMEM((chunks, 5, members // 2, 2, block, LANES), jnp.float32),
            *arrive,
            pltpu.VMEM((chunks - subs, 5, 1, block, LANES), jnp.float32),
            pltpu.SemaphoreType.DMA((bits, chunks)),
            pltpu.SemaphoreType.DMA((bits, chunks)),
            pltpu.SemaphoreType.DMA((chunks - subs,)),
            pltpu.SemaphoreType.DMA((chunks - subs,)),
        ],
        compiler_params=pltpu.CompilerParams(
            collective_id=0, has_side_effects=True, vmem_limit_bytes=60 * 1024 * 1024),
        cost_estimate=pl.CostEstimate(
            flops=40 * slices * rows * cols, bytes_accessed=level_set.size * 2,
            transcendentals=2 * slices * rows * cols),
    )(level_set, ray_length, member_flip, group_flip)
    if subs > 1:
        image = image.reshape(5, subs, pixels // cols, cols // subs).transpose(0, 2, 1, 3)
    return image.reshape(5, pixels)


def solution(mesh):
    in_specs = (P(("group", "member"), None, None), P(), P("group"), P())
    out_specs = P(None, ("group", "member"))
    run = functools.partial(body, mesh.shape["group"], mesh.shape["member"])
    return jax.shard_map(run, mesh=mesh, in_specs=in_specs, out_specs=out_specs, check_vma=False)
```

```python
import functools
import math

import jax
import jax.numpy as jnp
from jax import lax
from jax.experimental import pallas as pl
from jax.experimental.pallas import tpu as pltpu
from jax.sharding import PartitionSpec as P

MESH = pl.DeviceIdType.MESH
LANES = 128
PAD = 8


def flip_bit(index, bit):
    own = (index // (1 << bit)) % 2
    return index + (1 - 2 * own) * (1 << bit), own


def kernel(cfg, level_ref, ray_ref, mflip_ref, gflip_ref, out_ref,
           level_here, ray_here, fetch_sem, ray_sem, lev, part, *rest):
    groups, members, bits, slices, rows, cols, subs, block = cfg
    depths = slices * members * groups
    arrive, clear_in, sums = rest[0], rest[1:bits], rest[bits:2 * bits]
    from_group, send_sem, recv_sem, sum_send, sum_recv, gsend_sem, grecv_sem = rest[2 * bits:]
    chunks = groups * subs
    chunk_rows = rows // groups
    chunk_cols = cols // subs
    tiles_wide = chunk_cols // LANES
    width = min(512, chunk_cols)

    group_id = lax.axis_index("group")
    member_id = lax.axis_index("member")
    whole_flip = gflip_ref[0]
    member_mask = jnp.bitwise_xor(mflip_ref[0], whole_flip % members)
    group_mask = whole_flip // members
    member_rank = jnp.bitwise_xor(member_id, member_mask)
    group_rank = jnp.bitwise_xor(group_id, group_mask)
    first = (group_rank * members + member_rank) * slices

    barrier = pltpu.get_barrier_semaphore()
    for bit in range(bits):
        partner, _ = flip_bit(member_id, bit)
        pl.semaphore_signal(barrier, inc=1, device_id=(group_id, partner), device_id_type=MESH)
    for step in range(groups - 1):
        other = (group_id + 1 + step) % groups
        pl.semaphore_signal(barrier, inc=1, device_id=(other, member_id), device_id_type=MESH)

    strips = rows // 16
    start_row = ((group_id + 1) % groups) * chunk_rows
    first_strip = (start_row + chunk_rows % 16) // 16 + strips - 1
    early = min(chunk_rows // 16 + 2, strips)

    def strip_row(p):
        return pl.multiple_of(((first_strip + p) % strips) * 16, 16)

    def fetch(p):
        at = pl.ds(strip_row(p), 16)
        return pltpu.make_async_copy(level_ref.at[:, at, :], level_here.at[:, at, :], fetch_sem.at[p])

    rays = pltpu.make_async_copy(ray_ref, ray_here, ray_sem)
    for p in range(early):
        fetch(p).start()
    rays.start()
    for p in range(early, strips):
        fetch(p).start()

    def unpack(p):
        fetch(p).wait()
        r = strip_row(p)
        for k in range(slices):
            value = level_here[k, pl.ds(r, 16), :].astype(jnp.float32)
            at = pl.ds(pl.multiple_of(r + PAD, 8), 16)
            lev[k, at, LANES:LANES + cols] = value
            lev[k, at, 0:LANES] = jnp.broadcast_to(value[:, 0:1], (16, LANES))
            lev[k, at, LANES + cols:] = jnp.broadcast_to(value[:, cols - 1:cols], (16, LANES))

        @pl.when(r == 0)
        def _():
            for k in range(slices):
                lev[k, 0:PAD, :] = jnp.broadcast_to(
                    lev[k, PAD:PAD + 1, :], (PAD, cols + 2 * LANES))

        @pl.when(r == rows - 16)
        def _():
            for k in range(slices):
                lev[k, PAD + rows:, :] = jnp.broadcast_to(
                    lev[k, PAD + rows - 1:PAD + rows, :], (PAD, cols + 2 * LANES))

    period = slices * members
    base_phase = (2.0 * math.pi / period) * (first % period).astype(jnp.float32)
    band = []
    for c in range(3):
        angle = jnp.full((8, LANES), base_phase + 2.0 * math.pi / 3.0 * c, jnp.float32)
        band.append((0.5 * jnp.cos(angle), 0.5 * jnp.sin(angle)))
    first_real = first.astype(jnp.float32)

    def march(t):
        target = (group_id + 1 + t % groups) % groups
        sub = t // groups
        flat = part.at[t].reshape(5, members * block, LANES)

        @pl.loop(0, (chunk_rows // 8) * (chunk_cols // width))
        def _(i):
            local = (i // (chunk_cols // width)) * 8
            local_col = (i % (chunk_cols // width)) * width
            r0 = pl.multiple_of(target * chunk_rows + local, 8)
            c0 = pl.multiple_of(sub * chunk_cols + local_col, LANES)
            left_samples = ray_here[pl.ds(r0, 8), pl.ds(c0, width)] - first
            through = jnp.ones((8, width), jnp.float32)
            plain = jnp.zeros((8, width), jnp.float32)
            even = odd = distance = plain
            for k in range(slices):
                wide = lev[k, pl.ds(pl.multiple_of(r0 + PAD, 8), 8), pl.ds(c0, width + 2 * LANES)]
                total = width + 2 * LANES
                left = pltpu.roll(wide, 1, 1)[:, LANES:LANES + width]
                right = pltpu.roll(wide, total - 1, 1)[:, LANES:LANES + width]
                phi = wide[:, LANES:LANES + width]
                tall = lev[k, pl.ds(r0, 24), pl.ds(pl.multiple_of(c0 + LANES, LANES), width)]
                across = right - left
                downward = tall[9:17] - tall[7:15]
                facing = (0.48 * across + 0.6 * downward + 1.28) * lax.rsqrt(
                    across * across + downward * downward + 4.0)
                shading = 0.25 + 0.75 * jnp.maximum(facing, 0.0)
                opacity = jnp.exp2(phi * phi * (-4.0 / math.log(2.0)) + math.log2(9.0 / depths))
                opacity = jnp.where(left_samples > k, opacity, 0.0)
                weight = through * opacity
                through = through - weight
                distance = distance + weight * ((first_real + (k + 0.5)) / depths)
                shaded = weight * shading
                plain = plain + shaded
                even = even + shaded * math.cos(2.0 * math.pi * k / period)
                if k:
                    odd = odd + shaded * math.sin(2.0 * math.pi * k / period)
            for j in range(width // LANES):
                cut = slice(j * LANES, (j + 1) * LANES)
                at = pl.ds(local * tiles_wide + local_col // LANES + j, 8, stride=tiles_wide)
                for c in range(3):
                    flat[c, at, :] = (0.5 * plain[:, cut] + band[c][0] * even[:, cut]
                                      - band[c][1] * odd[:, cut])
                flat[3, at, :] = distance[:, cut]
                flat[4, at, :] = through[:, cut]

    def partner_of(bit):
        partner, own = flip_bit(member_id, bit)
        mine_front = jnp.bitwise_and(jnp.right_shift(member_rank, bit), 1) == 0
        return (group_id, partner), own, mine_front

    def swap(bit, t):
        partner, own, _ = partner_of(bit)
        if bit == 0:
            source, target = part.at[t, :, :, 1 - own], arrive.at[t]
        else:
            source = arrive.at[t, 4] if bit == 1 else clear_in[bit - 2].at[t]
            target = clear_in[bit - 1].at[t]
        return pltpu.make_async_remote_copy(
            src_ref=source, dst_ref=target,
            send_sem=send_sem.at[bit, t], recv_sem=recv_sem.at[bit, t],
            device_id=partner, device_id_type=MESH)

    def slot(t):
        return (t // groups) * (groups - 1) + t % groups

    def hand_over(t):
        target = (group_id + 1 + t % groups) % groups
        return pltpu.make_async_remote_copy(
            src_ref=arrive.at[t], dst_ref=from_group.at[slot(t)],
            send_sem=gsend_sem.at[slot(t)], recv_sem=grecv_sem.at[slot(t)],
            device_id=(target, member_id), device_id_type=MESH)

    def blend_cores(t):
        _, own, mine_front = partner_of(0)
        swap(0, t).wait_recv()

        @pl.loop(0, members // 2)
        def _(z):
            mine, theirs = part[t, 4, z, own], arrive[t, 4, z]
            keep_scale = jnp.where(mine_front, 1.0, theirs)
            come_scale = jnp.where(mine_front, mine, 1.0)
            for c in range(4):
                arrive[t, c, z] = keep_scale * part[t, c, z, own] + come_scale * arrive[t, c, z]
            arrive[t, 4, z] = mine * theirs

    def attenuate(bit, t):
        _, _, mine_front = partner_of(bit)
        swap(bit, t).wait_recv()
        if bit == bits - 1:
            swap(1, t).wait_send()

        @pl.loop(0, members // 2)
        def _(z):
            mine = arrive[t, 4, z] if bit == 1 else clear_in[bit - 2][t, z]
            theirs = clear_in[bit - 1][t, z]
            scale = jnp.where(mine_front, 1.0, theirs)
            for c in range(4):
                arrive[t, c, z] = scale * arrive[t, c, z]
            if bit < bits - 1:
                clear_in[bit - 1][t, z] = mine * theirs
            else:
                arrive[t, 4, z] = mine * theirs

    def summed(level, s):
        return sums[level].at[s].reshape(4, members >> (level + 1), block, LANES)

    def sum_swap(bit, s):
        partner, own, _ = partner_of(bit)
        return pltpu.make_async_remote_copy(
            src_ref=sums[bit - 1].at[s, :, :, 1 - own], dst_ref=summed(bit, s),
            send_sem=sum_send.at[bit, s], recv_sem=sum_recv.at[bit, s],
            device_id=partner, device_id_type=MESH)

    def put(c, s, value):
        for q in range(block):
            at = (q // tiles_wide) * cols + (q % tiles_wide) * LANES
            at = pl.ds(pl.multiple_of(s * chunk_cols + at, LANES), LANES)
            out_ref[c:c + 1, at] = value[q:q + 1, :]

    senders = [(group_id + 2 * groups - 1 - i) % groups for i in range(groups)]
    ranks = [jnp.bitwise_xor(s, group_mask) for s in senders]

    def merge_groups(s):
        for i in range(groups - 1):
            hand_over(s * groups + i).wait_recv()

        def piece(i, c, z):
            if i < groups - 1:
                return from_group[s * (groups - 1) + i, c, z]
            return arrive[s * groups + i, c, z]
        target = summed(0, s)

        @pl.loop(0, members // 2)
        def _(z):
            clear = [piece(i, 4, z) for i in range(groups)]
            total = [None] * 4
            for i in range(groups):
                ahead = None
                for h in range(groups):
                    if h != i:
                        term = jnp.where(ranks[h] < ranks[i], clear[h], 1.0)
                        ahead = term if ahead is None else ahead * term
                for c in range(4):
                    term = ahead * piece(i, c, z)
                    total[c] = term if total[c] is None else total[c] + term
            for c in range(4):
                target[c, z] = total[c]

            @pl.when(z == member_id // 2)
            def _():
                put(4, s, 1.0 - functools.reduce(lambda a, b: a * b, clear))

    def add_up(bit, s):
        _, own, _ = partner_of(bit)
        sum_swap(bit, s).wait_recv()
        target = summed(bit, s)
        if bit == bits - 1:
            for c in range(4):
                put(c, s, sums[bit - 1][s, c, 0, own] + target[c, 0])
        else:
            @pl.loop(0, members >> (bit + 1))
            def _(z):
                for c in range(4):
                    target[c, z] = target[c, z] + sums[bit - 1][s, c, z, own]

    pl.loop(0, early)(unpack)
    rays.wait()
    march(0)
    pl.semaphore_wait(barrier, bits + groups - 1)

    delay = [2 * bit for bit in range(2 * bits)]

    @pl.loop(0, chunks + delay[-1])
    def _(t):
        @pl.when(t < chunks)
        def _():
            swap(0, t).start()

        @pl.when(t == 0)
        def _():
            pl.loop(early, strips)(unpack)

        @pl.when(t < chunks - 1)
        def _():
            march(t + 1)
        for bit in range(bits):
            now = t - delay[bit]

            @pl.when((now >= 0) & (now < chunks))
            def _():
                if bit == 0:
                    blend_cores(now)
                else:
                    attenuate(bit, now)
                if bit < bits - 1:
                    swap(bit + 1, now).start()
                else:
                    @pl.when(now % groups != groups - 1)
                    def _():
                        hand_over(now).start()

        for bit in range(bits):
            now = t - delay[bits + bit]

            @pl.when((now >= 0) & (now < chunks) & (now % groups == groups - 1))
            def _():
                cut = now // groups
                if bit == 0:
                    merge_groups(cut)
                else:
                    add_up(bit, cut)
                if bit < bits - 1:
                    sum_swap(bit + 1, cut).start()

    @pl.loop(0, chunks)
    def _(t):
        for bit in range(bits):
            if bit != 1:
                swap(bit, t).wait_send()

        @pl.when(t % groups != groups - 1)
        def _():
            hand_over(t).wait_send()

    @pl.loop(0, subs)
    def _(s):
        for bit in range(1, bits):
            sum_swap(bit, s).wait_send()


def body(groups, members, level_set, ray_length, member_flip, group_flip):
    slices, rows, cols = level_set.shape
    bits = members.bit_length() - 1
    pixels = rows * cols // (groups * members)
    whole_rows = pixels % cols == 0
    subs = 1
    while whole_rows and subs < 4 and pixels % (2 * subs * 8 * LANES) == 0:
        subs *= 2
    block = pixels // LANES // subs
    chunks = groups * subs
    cfg = (groups, members, bits, slices, rows, cols, subs, block)
    half = members // 2
    sums = []
    for bit in range(bits):
        count = members >> (bit + 1)
        shape = (count // 2, 2) if bit < bits - 1 else (1,)
        sums.append(pltpu.VMEM((subs, 4) + shape + (block, LANES), jnp.float32))
    vmem = pl.BlockSpec(memory_space=pltpu.VMEM)
    anywhere = pl.BlockSpec(memory_space=pl.ANY)
    smem = pl.BlockSpec(memory_space=pltpu.SMEM)
    return pl.pallas_call(
        functools.partial(kernel, cfg),
        out_shape=jax.ShapeDtypeStruct((5, pixels), jnp.float32),
        in_specs=[anywhere, anywhere, smem, smem],
        out_specs=vmem,
        scratch_shapes=[
            pltpu.VMEM((slices, rows, cols), level_set.dtype),
            pltpu.VMEM((rows, cols), ray_length.dtype),
            pltpu.SemaphoreType.DMA((rows // 16,)),
            pltpu.SemaphoreType.DMA,
            pltpu.VMEM((slices, rows + 2 * PAD, cols + 2 * LANES), jnp.float32),
            pltpu.VMEM((chunks, 5, members // 2, 2, block, LANES), jnp.float32),
            pltpu.VMEM((chunks, 5, half, block, LANES), jnp.float32),
            *[pltpu.VMEM((chunks, half, block, LANES), jnp.float32)] * (bits - 1),
            *sums,
            pltpu.VMEM((chunks - subs, 5, half, block, LANES), jnp.float32),
            *[pltpu.SemaphoreType.DMA((bits, chunks))] * 2,
            *[pltpu.SemaphoreType.DMA((bits, subs))] * 2,
            *[pltpu.SemaphoreType.DMA((chunks - subs,))] * 2,
        ],
        compiler_params=pltpu.CompilerParams(
            collective_id=0, has_side_effects=True, vmem_limit_bytes=60 * 1024 * 1024),
        cost_estimate=pl.CostEstimate(
            flops=40 * slices * rows * cols, bytes_accessed=level_set.size * 2,
            transcendentals=2 * slices * rows * cols),
    )(level_set, ray_length, member_flip, group_flip)


def solution(mesh):
    in_specs = (P(("group", "member"), None, None), P(), P("group"), P())
    out_specs = P(None, ("group", "member"))
    run = functools.partial(body, mesh.shape["group"], mesh.shape["member"])
    return jax.shard_map(run, mesh=mesh, in_specs=in_specs, out_specs=out_specs, check_vma=False)
```

```python
import functools
import math

import jax
import jax.numpy as jnp
from jax import lax
from jax.experimental import pallas as pl
from jax.experimental.pallas import tpu as pltpu
from jax.sharding import PartitionSpec as P

MESH = pl.DeviceIdType.MESH
LANES = 128
PAD = 16


def flip_bit(index, bit):
    own = (index // (1 << bit)) % 2
    return index + (1 - 2 * own) * (1 << bit), own


def kernel(cfg, level_ref, ray_ref, mflip_ref, gflip_ref, out_ref,
           level_here, ray_here, fetch_sem, ray_sem, across_held, down_held, part, *rest):
    groups, members, bits, slices, rows, cols, subs, block = cfg
    depths = slices * members * groups
    arrive, clear_in, sums = rest[0], rest[1:bits], rest[bits:2 * bits]
    from_group, send_sem, recv_sem, sum_send, sum_recv, gsend_sem, grecv_sem = rest[2 * bits:]
    chunks = groups * subs
    chunk_rows = rows // groups
    chunk_cols = cols // subs
    tiles_wide = chunk_cols // LANES

    group_id = lax.axis_index("group")
    member_id = lax.axis_index("member")
    whole_flip = gflip_ref[0]
    member_mask = jnp.bitwise_xor(mflip_ref[0], whole_flip % members)
    group_mask = whole_flip // members
    member_rank = jnp.bitwise_xor(member_id, member_mask)
    group_rank = jnp.bitwise_xor(group_id, group_mask)
    first = (group_rank * members + member_rank) * slices

    barrier = pltpu.get_barrier_semaphore()
    for bit in range(bits):
        partner, _ = flip_bit(member_id, bit)
        pl.semaphore_signal(barrier, inc=1, device_id=(group_id, partner), device_id_type=MESH)
    for step in range(groups - 1):
        other = (group_id + 1 + step) % groups
        pl.semaphore_signal(barrier, inc=1, device_id=(other, member_id), device_id_type=MESH)

    strips = rows // 16
    start_row = ((group_id + 1) % groups) * chunk_rows
    first_strip = start_row // 16 + strips - 1
    early = min(max(chunk_rows // 16, 1) + 2, strips)

    def strip_row(p):
        return pl.multiple_of(((first_strip + p) % strips) * 16, 16)

    def fetch(p):
        at = pl.ds(strip_row(p), 16)
        return pltpu.make_async_copy(level_ref.at[:, at, :],
            level_here.at[:, pl.ds(strip_row(p) + PAD, 16), pl.ds(LANES, cols)], fetch_sem.at[p])

    rays = pltpu.make_async_copy(ray_ref, ray_here, ray_sem)
    for p in range(early):
        fetch(p).start()
    rays.start()
    for p in range(early, strips):
        fetch(p).start()

    def unpack(p):
        fetch(p).wait()
        r = strip_row(p)
        at = pl.ds(pl.multiple_of(r + PAD, 16), 16)
        for k in range(slices):
            start = level_here[k, at, LANES:2 * LANES].astype(jnp.float32)[:, 0:1]
            end = level_here[k, at, cols:cols + LANES].astype(jnp.float32)[:, LANES - 1:LANES]
            level_here[k, at, 0:LANES] = jnp.broadcast_to(start, (16, LANES)).astype(jnp.bfloat16)
            level_here[k, at, LANES + cols:] = jnp.broadcast_to(end, (16, LANES)).astype(jnp.bfloat16)

        @pl.when(r == 0)
        def _():
            for k in range(slices):
                edge = level_here[k, PAD:PAD + 16, :].astype(jnp.float32)[0:1]
                level_here[k, 0:PAD, :] = jnp.broadcast_to(
                    edge, (PAD, cols + 2 * LANES)).astype(jnp.bfloat16)

        @pl.when(r == rows - 16)
        def _():
            for k in range(slices):
                edge = level_here[k, rows:PAD + rows, :].astype(jnp.float32)[15:16]
                level_here[k, PAD + rows:, :] = jnp.broadcast_to(
                    edge, (PAD, cols + 2 * LANES)).astype(jnp.bfloat16)

    def differences(shape, near, far, offset):
        a = lax.broadcasted_iota(jnp.int32, shape, near)
        b = lax.broadcasted_iota(jnp.int32, shape, far) - offset
        up = jnp.where(b == a + 1, 1.0, 0.0)
        return (up - jnp.where(b == a - 1, 1.0, 0.0)).astype(jnp.bfloat16)

    span = min(256, chunk_cols)
    lane_matrix = differences((span + 2 * LANES, span), 1, 0, LANES)
    tall = max(chunk_rows, 16)
    high = min(chunk_rows, 16)
    width = min(4096 // high, chunk_cols)

    period = slices * members
    base_phase = (2.0 * math.pi / period) * (first % period).astype(jnp.float32)
    band = []
    for c in range(3):
        angle = jnp.full((min(chunk_rows, 16), LANES), base_phase + 2.0 * math.pi / 3.0 * c, jnp.float32)
        band.append((0.5 * jnp.cos(angle), 0.5 * jnp.sin(angle)))
    first_real = first.astype(jnp.float32)

    def march(t):
        target = (group_id + 1 + t % groups) % groups
        sub = t // groups
        flat = part.at[t].reshape(5, members * block, LANES)

        row0 = target * chunk_rows
        base = pl.multiple_of((row0 // 16) * 16, 16)
        offset = row0 % 16
        c_first = pl.multiple_of(sub * chunk_cols, LANES)
        row_matrix = differences((chunk_rows, tall + 32), 0, 1, PAD + offset)

        def own_rows(value):
            if chunk_rows % 16 == 0:
                return value
            return jnp.where(offset == 0, value[0:8], value[8:16])

        @pl.loop(0, slices)
        def _(k):
            for j in range(chunk_cols // span):
                here = slice(j * span, (j + 1) * span)
                at = pl.multiple_of(c_first + j * span, LANES)
                window = level_here[k, pl.ds(base + PAD, tall), pl.ds(at, span + 2 * LANES)]
                across_held[k, :, here] = own_rows(
                    jnp.dot(window, lane_matrix, preferred_element_type=jnp.float32))
                window = level_here[k, pl.ds(base, tall + 32), pl.ds(at + LANES, span)]
                down_held[k, :, here] = jnp.dot(
                    row_matrix, window, preferred_element_type=jnp.float32)

        @pl.loop(0, (chunk_rows // high) * (chunk_cols // width))
        def _(i):
            local = pl.multiple_of((i // (chunk_cols // width)) * high, high)
            local_col = pl.multiple_of((i % (chunk_cols // width)) * width, LANES)
            r0 = pl.multiple_of(row0 + local, 8)
            c0 = pl.multiple_of(c_first + local_col, LANES)
            left_samples = ray_here[pl.ds(r0, high), pl.ds(c0, width)] - first
            through = jnp.ones((high, width), jnp.float32)
            plain = jnp.zeros((high, width), jnp.float32)
            even = odd = distance = plain
            for k in range(slices):
                phi = own_rows(level_here[
                    k, pl.ds(pl.multiple_of(base + PAD + local, 16), 16),
                    pl.ds(c0 + LANES, width)].astype(jnp.float32))
                across = across_held[k, pl.ds(local, high), pl.ds(local_col, width)]
                downward = down_held[k, pl.ds(local, high), pl.ds(local_col, width)]
                facing = (0.48 * across + 0.6 * downward + 1.28) * lax.rsqrt(
                    across * across + downward * downward + 4.0)
                shading = 0.25 + 0.75 * jnp.maximum(facing, 0.0)
                opacity = jnp.exp2(phi * phi * (-4.0 / math.log(2.0)) + math.log2(9.0 / depths))
                opacity = jnp.where(left_samples > k, opacity, 0.0)
                weight = through * opacity
                through = through - weight
                distance = distance + weight * ((first_real + (k + 0.5)) / depths)
                shaded = weight * shading
                plain = plain + shaded
                even = even + shaded * math.cos(2.0 * math.pi * k / period)
                if k:
                    odd = odd + shaded * math.sin(2.0 * math.pi * k / period)
            for j in range(width // LANES):
                cut = slice(j * LANES, (j + 1) * LANES)
                at = pl.ds(local * tiles_wide + local_col // LANES + j, high, stride=tiles_wide)
                for c in range(3):
                    flat[c, at, :] = (0.5 * plain[:, cut] + band[c][0] * even[:, cut]
                                      - band[c][1] * odd[:, cut])
                flat[3, at, :] = distance[:, cut]
                flat[4, at, :] = through[:, cut]

    def partner_of(bit):
        partner, own = flip_bit(member_id, bit)
        mine_front = jnp.bitwise_and(jnp.right_shift(member_rank, bit), 1) == 0
        return (group_id, partner), own, mine_front

    def swap(bit, t):
        partner, own, _ = partner_of(bit)
        if bit == 0:
            source, target = part.at[t, :, :, 1 - own], arrive.at[t]
        else:
            source = arrive.at[t, 4] if bit == 1 else clear_in[bit - 2].at[t]
            target = clear_in[bit - 1].at[t]
        return pltpu.make_async_remote_copy(
            src_ref=source, dst_ref=target,
            send_sem=send_sem.at[bit, t], recv_sem=recv_sem.at[bit, t],
            device_id=partner, device_id_type=MESH)

    def slot(t):
        return (t // groups) * (groups - 1) + t % groups

    def hand_over(t):
        target = (group_id + 1 + t % groups) % groups
        return pltpu.make_async_remote_copy(
            src_ref=arrive.at[t], dst_ref=from_group.at[slot(t)],
            send_sem=gsend_sem.at[slot(t)], recv_sem=grecv_sem.at[slot(t)],
            device_id=(target, member_id), device_id_type=MESH)

    def blend_cores(t):
        _, own, mine_front = partner_of(0)
        swap(0, t).wait_recv()

        @pl.loop(0, members // 2)
        def _(z):
            mine, theirs = part[t, 4, z, own], arrive[t, 4, z]
            keep_scale = jnp.where(mine_front, 1.0, theirs)
            come_scale = jnp.where(mine_front, mine, 1.0)
            for c in range(4):
                arrive[t, c, z] = keep_scale * part[t, c, z, own] + come_scale * arrive[t, c, z]
            arrive[t, 4, z] = mine * theirs

    def attenuate(bit, t):
        _, _, mine_front = partner_of(bit)
        swap(bit, t).wait_recv()
        if bit == bits - 1:
            swap(1, t).wait_send()

        @pl.loop(0, members // 2)
        def _(z):
            mine = arrive[t, 4, z] if bit == 1 else clear_in[bit - 2][t, z]
            theirs = clear_in[bit - 1][t, z]
            scale = jnp.where(mine_front, 1.0, theirs)
            for c in range(4):
                arrive[t, c, z] = scale * arrive[t, c, z]
            if bit < bits - 1:
                clear_in[bit - 1][t, z] = mine * theirs
            else:
                arrive[t, 4, z] = mine * theirs

    def summed(level, s):
        return sums[level].at[s].reshape(4, members >> (level + 1), block, LANES)

    def sum_swap(bit, s):
        partner, own, _ = partner_of(bit)
        return pltpu.make_async_remote_copy(
            src_ref=sums[bit - 1].at[s, :, :, 1 - own], dst_ref=summed(bit, s),
            send_sem=sum_send.at[bit, s], recv_sem=sum_recv.at[bit, s],
            device_id=partner, device_id_type=MESH)

    def put(c, s, value):
        for q in range(block):
            at = (q // tiles_wide) * cols + (q % tiles_wide) * LANES
            at = pl.ds(pl.multiple_of(s * chunk_cols + at, LANES), LANES)
            out_ref[c:c + 1, at] = value[q:q + 1, :]

    senders = [(group_id + 2 * groups - 1 - i) % groups for i in range(groups)]
    ranks = [jnp.bitwise_xor(s, group_mask) for s in senders]

    def merge_groups(s):
        for i in range(groups - 1):
            hand_over(s * groups + i).wait_recv()

        def piece(i, c, z):
            if i < groups - 1:
                return from_group[s * (groups - 1) + i, c, z]
            return arrive[s * groups + i, c, z]
        target = summed(0, s)

        @pl.loop(0, members // 2)
        def _(z):
            clear = [piece(i, 4, z) for i in range(groups)]
            total = [None] * 4
            for i in range(groups):
                ahead = None
                for h in range(groups):
                    if h != i:
                        term = jnp.where(ranks[h] < ranks[i], clear[h], 1.0)
                        ahead = term if ahead is None else ahead * term
                for c in range(4):
                    term = ahead * piece(i, c, z)
                    total[c] = term if total[c] is None else total[c] + term
            for c in range(4):
                target[c, z] = total[c]

            @pl.when(z == member_id // 2)
            def _():
                put(4, s, 1.0 - functools.reduce(lambda a, b: a * b, clear))

    def add_up(bit, s):
        _, own, _ = partner_of(bit)
        sum_swap(bit, s).wait_recv()
        target = summed(bit, s)
        if bit == bits - 1:
            for c in range(4):
                put(c, s, sums[bit - 1][s, c, 0, own] + target[c, 0])
        else:
            @pl.loop(0, members >> (bit + 1))
            def _(z):
                for c in range(4):
                    target[c, z] = target[c, z] + sums[bit - 1][s, c, z, own]

    pl.loop(0, early)(unpack)
    rays.wait()
    march(0)
    pl.semaphore_wait(barrier, bits + groups - 1)

    delay = [2 * bit for bit in range(2 * bits)]

    @pl.loop(0, chunks + delay[-1])
    def _(t):
        @pl.when(t < chunks)
        def _():
            swap(0, t).start()

        @pl.when(t == 0)
        def _():
            pl.loop(early, strips)(unpack)

        @pl.when(t < chunks - 1)
        def _():
            march(t + 1)
        for bit in range(bits):
            now = t - delay[bit]

            @pl.when((now >= 0) & (now < chunks))
            def _():
                if bit == 0:
                    blend_cores(now)
                else:
                    attenuate(bit, now)
                if bit < bits - 1:
                    swap(bit + 1, now).start()
                else:
                    @pl.when(now % groups != groups - 1)
                    def _():
                        hand_over(now).start()

        for bit in range(bits):
            now = t - delay[bits + bit]

            @pl.when((now >= 0) & (now < chunks) & (now % groups == groups - 1))
            def _():
                cut = now // groups
                if bit == 0:
                    merge_groups(cut)
                else:
                    add_up(bit, cut)
                if bit < bits - 1:
                    sum_swap(bit + 1, cut).start()

    @pl.loop(0, chunks)
    def _(t):
        for bit in range(bits):
            if bit != 1:
                swap(bit, t).wait_send()

        @pl.when(t % groups != groups - 1)
        def _():
            hand_over(t).wait_send()

    @pl.loop(0, subs)
    def _(s):
        for bit in range(1, bits):
            sum_swap(bit, s).wait_send()


def body(groups, members, level_set, ray_length, member_flip, group_flip):
    slices, rows, cols = level_set.shape
    bits = members.bit_length() - 1
    pixels = rows * cols // (groups * members)
    whole_rows = pixels % cols == 0
    subs = 1
    while whole_rows and subs < 4 and pixels % (2 * subs * 8 * LANES) == 0:
        subs *= 2
    block = pixels // LANES // subs
    chunks = groups * subs
    cfg = (groups, members, bits, slices, rows, cols, subs, block)
    half = members // 2
    sums = []
    for bit in range(bits):
        count = members >> (bit + 1)
        shape = (count // 2, 2) if bit < bits - 1 else (1,)
        sums.append(pltpu.VMEM((subs, 4) + shape + (block, LANES), jnp.float32))
    vmem = pl.BlockSpec(memory_space=pltpu.VMEM)
    anywhere = pl.BlockSpec(memory_space=pl.ANY)
    smem = pl.BlockSpec(memory_space=pltpu.SMEM)
    return pl.pallas_call(
        functools.partial(kernel, cfg),
        out_shape=jax.ShapeDtypeStruct((5, pixels), jnp.float32),
        in_specs=[anywhere, anywhere, smem, smem],
        out_specs=vmem,
        scratch_shapes=[
            pltpu.VMEM((slices, rows + 2 * PAD, cols + 2 * LANES), level_set.dtype),
            pltpu.VMEM((rows, cols), ray_length.dtype),
            pltpu.SemaphoreType.DMA((rows // 16,)),
            pltpu.SemaphoreType.DMA,
            *[pltpu.VMEM((slices, rows // groups, cols // subs), jnp.float32)] * 2,
            pltpu.VMEM((chunks, 5, members // 2, 2, block, LANES), jnp.float32),
            pltpu.VMEM((chunks, 5, half, block, LANES), jnp.float32),
            *[pltpu.VMEM((chunks, half, block, LANES), jnp.float32)] * (bits - 1),
            *sums,
            pltpu.VMEM((chunks - subs, 5, half, block, LANES), jnp.float32),
            *[pltpu.SemaphoreType.DMA((bits, chunks))] * 2,
            *[pltpu.SemaphoreType.DMA((bits, subs))] * 2,
            *[pltpu.SemaphoreType.DMA((chunks - subs,))] * 2,
        ],
        compiler_params=pltpu.CompilerParams(
            collective_id=0, has_side_effects=True, vmem_limit_bytes=60 * 1024 * 1024),
        cost_estimate=pl.CostEstimate(
            flops=40 * slices * rows * cols, bytes_accessed=level_set.size * 2,
            transcendentals=2 * slices * rows * cols),
    )(level_set, ray_length, member_flip, group_flip)


def solution(mesh):
    in_specs = (P(("group", "member"), None, None), P(), P("group"), P())
    out_specs = P(None, ("group", "member"))
    run = functools.partial(body, mesh.shape["group"], mesh.shape["member"])
    return jax.shard_map(run, mesh=mesh, in_specs=in_specs, out_specs=out_specs, check_vma=False)
```

```python
import functools
import math

import jax
import jax.numpy as jnp
from jax import lax
from jax.experimental import pallas as pl
from jax.experimental.pallas import tpu as pltpu
from jax.sharding import PartitionSpec as P

MESH = pl.DeviceIdType.MESH
LANES = 128
PAD = 16


def flip_bit(index, bit):
    own = (index // (1 << bit)) % 2
    return index + (1 - 2 * own) * (1 << bit), own


def kernel(cfg, level_ref, ray_ref, mflip_ref, gflip_ref, out_ref,
           level_here, ray_here, fetch_sem, ray_sem, across_held, part, *rest):
    groups, members, bits, slices, rows, cols, subs, block = cfg
    depths = slices * members * groups
    arrive, clear_in, sums = rest[0], rest[1:bits], rest[bits:2 * bits]
    from_group, send_sem, recv_sem, sum_send, sum_recv, gsend_sem, grecv_sem = rest[2 * bits:]
    chunks = groups * subs
    chunk_rows = rows // groups
    chunk_cols = cols // subs
    tiles_wide = chunk_cols // LANES

    group_id = lax.axis_index("group")
    member_id = lax.axis_index("member")
    whole_flip = gflip_ref[0]
    member_mask = jnp.bitwise_xor(mflip_ref[0], whole_flip % members)
    group_mask = whole_flip // members
    member_rank = jnp.bitwise_xor(member_id, member_mask)
    group_rank = jnp.bitwise_xor(group_id, group_mask)
    first = (group_rank * members + member_rank) * slices

    barrier = pltpu.get_barrier_semaphore()
    for bit in range(bits):
        partner, _ = flip_bit(member_id, bit)
        pl.semaphore_signal(barrier, inc=1, device_id=(group_id, partner), device_id_type=MESH)
    for step in range(groups - 1):
        other = (group_id + 1 + step) % groups
        pl.semaphore_signal(barrier, inc=1, device_id=(other, member_id), device_id_type=MESH)

    strips = rows // 16
    start_row = ((group_id + 1) % groups) * chunk_rows
    first_strip = start_row // 16 + strips - 1
    early = min(max(chunk_rows // 16, 1) + 2, strips)

    def strip_row(p):
        return pl.multiple_of(((first_strip + p) % strips) * 16, 16)

    def fetch(p):
        at = pl.ds(strip_row(p), 16)
        return pltpu.make_async_copy(level_ref.at[:, at, :],
            level_here.at[:, pl.ds(strip_row(p) + PAD, 16), pl.ds(LANES, cols)], fetch_sem.at[p])

    rays = pltpu.make_async_copy(ray_ref, ray_here, ray_sem)
    for p in range(early):
        fetch(p).start()
    rays.start()
    for p in range(early, strips):
        fetch(p).start()

    def unpack(p):
        fetch(p).wait()
        r = strip_row(p)
        at = pl.ds(pl.multiple_of(r + PAD, 16), 16)
        for k in range(slices):
            start = level_here[k, at, LANES:2 * LANES].astype(jnp.float32)[:, 0:1]
            end = level_here[k, at, cols:cols + LANES].astype(jnp.float32)[:, LANES - 1:LANES]
            level_here[k, at, 0:LANES] = jnp.broadcast_to(start, (16, LANES)).astype(jnp.bfloat16)
            level_here[k, at, LANES + cols:] = jnp.broadcast_to(end, (16, LANES)).astype(jnp.bfloat16)

        @pl.when(r == 0)
        def _():
            for k in range(slices):
                edge = level_here[k, PAD:PAD + 16, :].astype(jnp.float32)[0:1]
                level_here[k, 0:PAD, :] = jnp.broadcast_to(
                    edge, (PAD, cols + 2 * LANES)).astype(jnp.bfloat16)

        @pl.when(r == rows - 16)
        def _():
            for k in range(slices):
                edge = level_here[k, rows:PAD + rows, :].astype(jnp.float32)[15:16]
                level_here[k, PAD + rows:, :] = jnp.broadcast_to(
                    edge, (PAD, cols + 2 * LANES)).astype(jnp.bfloat16)

    def differences(shape, near, far, offset):
        a = lax.broadcasted_iota(jnp.int32, shape, near)
        b = lax.broadcasted_iota(jnp.int32, shape, far) - offset
        up = jnp.where(b == a + 1, 1.0, 0.0)
        return (up - jnp.where(b == a - 1, 1.0, 0.0)).astype(jnp.bfloat16)

    span = min(256, chunk_cols)
    lane_matrix = differences((span + 2 * LANES, span), 1, 0, LANES)
    tall = max(chunk_rows, 16)
    high = chunk_rows
    width = max(LANES, 4096 // high)

    period = slices * members
    base_phase = (2.0 * math.pi / period) * (first % period).astype(jnp.float32)
    band = []
    for c in range(3):
        angle = jnp.full((chunk_rows, LANES), base_phase + 2.0 * math.pi / 3.0 * c, jnp.float32)
        band.append((0.5 * jnp.cos(angle), 0.5 * jnp.sin(angle)))
    first_real = first.astype(jnp.float32)

    def march(t):
        target = (group_id + 1 + t % groups) % groups
        sub = t // groups
        flat = part.at[t].reshape(5, members * block, LANES)

        row0 = target * chunk_rows
        base = pl.multiple_of((row0 // 16) * 16, 16)
        offset = row0 % 16
        c_first = pl.multiple_of(sub * chunk_cols, LANES)
        def own_rows(value):
            if chunk_rows % 16 == 0:
                return value
            return jnp.where(offset == 0, value[0:8], value[8:16])

        for j in range(chunk_cols // span):
            here = slice(j * span, (j + 1) * span)
            at = pl.multiple_of(c_first + j * span, LANES)
            window = level_here[:, pl.ds(base + PAD, tall), pl.ds(at, span + 2 * LANES)]
            across = jnp.dot(window.reshape(slices * tall, span + 2 * LANES), lane_matrix,
                             preferred_element_type=jnp.float32)
            for k in range(slices):
                across_held[k, :, here] = own_rows(across[k * tall:(k + 1) * tall])

        @pl.loop(0, (chunk_rows // high) * (chunk_cols // width))
        def _(i):
            local = (i // (chunk_cols // width)) * high
            local_col = pl.multiple_of((i % (chunk_cols // width)) * width, LANES)
            r0 = pl.multiple_of(row0 + local, 8)
            c0 = pl.multiple_of(c_first + local_col, LANES)
            left_samples = ray_here[pl.ds(r0, high), pl.ds(c0, width)] - first
            through = jnp.ones((high, width), jnp.float32)
            plain = jnp.zeros((high, width), jnp.float32)
            even = odd = distance = plain
            for k in range(slices):
                window = level_here[
                    k, pl.ds(pl.multiple_of(base + local, 16), tall + 32),
                    pl.ds(c0 + LANES, width)].astype(jnp.float32)
                phi = own_rows(window[PAD:PAD + tall])
                downward = own_rows(window[PAD + 1:PAD + 1 + tall]) - own_rows(
                    window[PAD - 1:PAD - 1 + tall])
                across = across_held[k, pl.ds(local, high), pl.ds(local_col, width)]
                facing = (0.48 * across + 0.6 * downward + 1.28) * lax.rsqrt(
                    across * across + downward * downward + 4.0)
                shading = 0.25 + 0.75 * jnp.maximum(facing, 0.0)
                opacity = jnp.exp2(phi * phi * (-4.0 / math.log(2.0)) + math.log2(9.0 / depths))
                opacity = jnp.where(left_samples > k, opacity, 0.0)
                weight = through * opacity
                through = through - weight
                distance = distance + weight * ((first_real + (k + 0.5)) / depths)
                shaded = weight * shading
                plain = plain + shaded
                even = even + shaded * math.cos(2.0 * math.pi * k / period)
                if k:
                    odd = odd + shaded * math.sin(2.0 * math.pi * k / period)
            for j in range(width // LANES):
                cut = slice(j * LANES, (j + 1) * LANES)
                at = pl.ds(local * tiles_wide + local_col // LANES + j, high, stride=tiles_wide)
                for c in range(3):
                    flat[c, at, :] = (0.5 * plain[:, cut] + band[c][0] * even[:, cut]
                                      - band[c][1] * odd[:, cut])
                flat[3, at, :] = distance[:, cut]
                flat[4, at, :] = through[:, cut]

    def partner_of(bit):
        partner, own = flip_bit(member_id, bit)
        mine_front = jnp.bitwise_and(jnp.right_shift(member_rank, bit), 1) == 0
        return (group_id, partner), own, mine_front

    def swap(bit, t):
        partner, own, _ = partner_of(bit)
        if bit == 0:
            source, target = part.at[t, :, :, 1 - own], arrive.at[t]
        else:
            source = arrive.at[t, 4] if bit == 1 else clear_in[bit - 2].at[t]
            target = clear_in[bit - 1].at[t]
        return pltpu.make_async_remote_copy(
            src_ref=source, dst_ref=target,
            send_sem=send_sem.at[bit, t], recv_sem=recv_sem.at[bit, t],
            device_id=partner, device_id_type=MESH)

    def slot(t):
        return (t // groups) * (groups - 1) + t % groups

    def hand_over(t):
        target = (group_id + 1 + t % groups) % groups
        return pltpu.make_async_remote_copy(
            src_ref=arrive.at[t], dst_ref=from_group.at[slot(t)],
            send_sem=gsend_sem.at[slot(t)], recv_sem=grecv_sem.at[slot(t)],
            device_id=(target, member_id), device_id_type=MESH)

    def blend_cores(t):
        _, own, mine_front = partner_of(0)
        swap(0, t).wait_recv()

        @pl.loop(0, members // 2)
        def _(z):
            mine, theirs = part[t, 4, z, own], arrive[t, 4, z]
            keep_scale = jnp.where(mine_front, 1.0, theirs)
            come_scale = jnp.where(mine_front, mine, 1.0)
            for c in range(4):
                arrive[t, c, z] = keep_scale * part[t, c, z, own] + come_scale * arrive[t, c, z]
            arrive[t, 4, z] = mine * theirs

    def attenuate(bit, t):
        _, _, mine_front = partner_of(bit)
        swap(bit, t).wait_recv()
        if bit == bits - 1:
            swap(1, t).wait_send()

        @pl.loop(0, members // 2)
        def _(z):
            mine = arrive[t, 4, z] if bit == 1 else clear_in[bit - 2][t, z]
            theirs = clear_in[bit - 1][t, z]
            scale = jnp.where(mine_front, 1.0, theirs)
            for c in range(4):
                arrive[t, c, z] = scale * arrive[t, c, z]
            if bit < bits - 1:
                clear_in[bit - 1][t, z] = mine * theirs
            else:
                arrive[t, 4, z] = mine * theirs

    def summed(level, s):
        return sums[level].at[s].reshape(4, members >> (level + 1), block, LANES)

    def sum_swap(bit, s):
        partner, own, _ = partner_of(bit)
        return pltpu.make_async_remote_copy(
            src_ref=sums[bit - 1].at[s, :, :, 1 - own], dst_ref=summed(bit, s),
            send_sem=sum_send.at[bit, s], recv_sem=sum_recv.at[bit, s],
            device_id=partner, device_id_type=MESH)

    def put(c, s, value):
        for q in range(block):
            at = (q // tiles_wide) * cols + (q % tiles_wide) * LANES
            at = pl.ds(pl.multiple_of(s * chunk_cols + at, LANES), LANES)
            out_ref[c:c + 1, at] = value[q:q + 1, :]

    senders = [(group_id + 2 * groups - 1 - i) % groups for i in range(groups)]
    ranks = [jnp.bitwise_xor(s, group_mask) for s in senders]

    def merge_groups(s):
        for i in range(groups - 1):
            hand_over(s * groups + i).wait_recv()

        def piece(i, c, z):
            if i < groups - 1:
                return from_group[s * (groups - 1) + i, c, z]
            return arrive[s * groups + i, c, z]
        target = summed(0, s)

        @pl.loop(0, members // 2)
        def _(z):
            clear = [piece(i, 4, z) for i in range(groups)]
            total = [None] * 4
            for i in range(groups):
                ahead = None
                for h in range(groups):
                    if h != i:
                        term = jnp.where(ranks[h] < ranks[i], clear[h], 1.0)
                        ahead = term if ahead is None else ahead * term
                for c in range(4):
                    term = ahead * piece(i, c, z)
                    total[c] = term if total[c] is None else total[c] + term
            for c in range(4):
                target[c, z] = total[c]

            @pl.when(z == member_id // 2)
            def _():
                put(4, s, 1.0 - functools.reduce(lambda a, b: a * b, clear))

    def add_up(bit, s):
        _, own, _ = partner_of(bit)
        sum_swap(bit, s).wait_recv()
        target = summed(bit, s)
        if bit == bits - 1:
            for c in range(4):
                put(c, s, sums[bit - 1][s, c, 0, own] + target[c, 0])
        else:
            @pl.loop(0, members >> (bit + 1))
            def _(z):
                for c in range(4):
                    target[c, z] = target[c, z] + sums[bit - 1][s, c, z, own]

    pl.loop(0, early)(unpack)
    rays.wait()
    march(0)
    pl.semaphore_wait(barrier, bits + groups - 1)

    delay = [2 * bit for bit in range(2 * bits)]

    @pl.loop(0, chunks + delay[-1])
    def _(t):
        @pl.when(t < chunks)
        def _():
            swap(0, t).start()

        @pl.when(t == 0)
        def _():
            pl.loop(early, strips)(unpack)

        @pl.when(t < chunks - 1)
        def _():
            march(t + 1)
        for bit in range(bits):
            now = t - delay[bit]

            @pl.when((now >= 0) & (now < chunks))
            def _():
                if bit == 0:
                    blend_cores(now)
                else:
                    attenuate(bit, now)
                if bit < bits - 1:
                    swap(bit + 1, now).start()
                else:
                    @pl.when(now % groups != groups - 1)
                    def _():
                        hand_over(now).start()

        for bit in range(bits):
            now = t - delay[bits + bit]

            @pl.when((now >= 0) & (now < chunks) & (now % groups == groups - 1))
            def _():
                cut = now // groups
                if bit == 0:
                    merge_groups(cut)
                else:
                    add_up(bit, cut)
                if bit < bits - 1:
                    sum_swap(bit + 1, cut).start()

    @pl.loop(0, chunks)
    def _(t):
        for bit in range(bits):
            if bit != 1:
                swap(bit, t).wait_send()

        @pl.when(t % groups != groups - 1)
        def _():
            hand_over(t).wait_send()

    @pl.loop(0, subs)
    def _(s):
        for bit in range(1, bits):
            sum_swap(bit, s).wait_send()


def body(groups, members, level_set, ray_length, member_flip, group_flip):
    slices, rows, cols = level_set.shape
    bits = members.bit_length() - 1
    pixels = rows * cols // (groups * members)
    whole_rows = pixels % cols == 0
    subs = 1
    while whole_rows and subs < 4 and pixels % (2 * subs * 8 * LANES) == 0:
        subs *= 2
    block = pixels // LANES // subs
    chunks = groups * subs
    cfg = (groups, members, bits, slices, rows, cols, subs, block)
    half = members // 2
    sums = []
    for bit in range(bits):
        count = members >> (bit + 1)
        shape = (count // 2, 2) if bit < bits - 1 else (1,)
        sums.append(pltpu.VMEM((subs, 4) + shape + (block, LANES), jnp.float32))
    vmem = pl.BlockSpec(memory_space=pltpu.VMEM)
    anywhere = pl.BlockSpec(memory_space=pl.ANY)
    smem = pl.BlockSpec(memory_space=pltpu.SMEM)
    return pl.pallas_call(
        functools.partial(kernel, cfg),
        out_shape=jax.ShapeDtypeStruct((5, pixels), jnp.float32),
        in_specs=[anywhere, anywhere, smem, smem],
        out_specs=vmem,
        scratch_shapes=[
            pltpu.VMEM((slices, rows + 2 * PAD, cols + 2 * LANES), level_set.dtype),
            pltpu.VMEM((rows, cols), ray_length.dtype),
            pltpu.SemaphoreType.DMA((rows // 16,)),
            pltpu.SemaphoreType.DMA,
            pltpu.VMEM((slices, rows // groups, cols // subs), jnp.float32),
            pltpu.VMEM((chunks, 5, members // 2, 2, block, LANES), jnp.float32),
            pltpu.VMEM((chunks, 5, half, block, LANES), jnp.float32),
            *[pltpu.VMEM((chunks, half, block, LANES), jnp.float32)] * (bits - 1),
            *sums,
            pltpu.VMEM((chunks - subs, 5, half, block, LANES), jnp.float32),
            *[pltpu.SemaphoreType.DMA((bits, chunks))] * 2,
            *[pltpu.SemaphoreType.DMA((bits, subs))] * 2,
            *[pltpu.SemaphoreType.DMA((chunks - subs,))] * 2,
        ],
        compiler_params=pltpu.CompilerParams(
            collective_id=0, has_side_effects=True, vmem_limit_bytes=60 * 1024 * 1024),
        cost_estimate=pl.CostEstimate(
            flops=40 * slices * rows * cols, bytes_accessed=level_set.size * 2,
            transcendentals=2 * slices * rows * cols),
    )(level_set, ray_length, member_flip, group_flip)


def solution(mesh):
    in_specs = (P(("group", "member"), None, None), P(), P("group"), P())
    out_specs = P(None, ("group", "member"))
    run = functools.partial(body, mesh.shape["group"], mesh.shape["member"])
    return jax.shard_map(run, mesh=mesh, in_specs=in_specs, out_specs=out_specs, check_vma=False)
```

```python
import functools
import math

import jax
import jax.numpy as jnp
from jax import lax
from jax.experimental import pallas as pl
from jax.experimental.pallas import tpu as pltpu
from jax.sharding import PartitionSpec as P

MESH = pl.DeviceIdType.MESH
LANES = 128
PAD = 8


def flip_bit(index, bit):
    own = (index // (1 << bit)) % 2
    return index + (1 - 2 * own) * (1 << bit), own


def kernel(cfg, level_ref, ray_ref, mflip_ref, gflip_ref, out_ref,
           level_here, ray_here, fetch_sem, ray_sem, lev, part, *rest):
    groups, members, bits, slices, rows, cols, subs, block = cfg
    depths = slices * members * groups
    arrive, from_group = rest[:bits], rest[bits]
    send_sem, recv_sem, gsend_sem, grecv_sem = rest[bits + 1:]
    chunks = groups * subs
    chunk_rows = rows // groups
    chunk_cols = cols // subs
    tiles_wide = chunk_cols // LANES
    width = min(512, chunk_cols)

    group_id = lax.axis_index("group")
    member_id = lax.axis_index("member")
    whole_flip = gflip_ref[0]
    member_mask = jnp.bitwise_xor(mflip_ref[0], whole_flip % members)
    group_mask = whole_flip // members
    member_rank = jnp.bitwise_xor(member_id, member_mask)
    group_rank = jnp.bitwise_xor(group_id, group_mask)
    first = (group_rank * members + member_rank) * slices

    barrier = pltpu.get_barrier_semaphore()
    for bit in range(bits):
        partner, _ = flip_bit(member_id, bit)
        pl.semaphore_signal(barrier, inc=1, device_id=(group_id, partner), device_id_type=MESH)
    for step in range(groups - 1):
        other = (group_id + 1 + step) % groups
        pl.semaphore_signal(barrier, inc=1, device_id=(other, member_id), device_id_type=MESH)

    strips = rows // 16
    start_row = ((group_id + 1) % groups) * chunk_rows
    first_strip = (start_row + chunk_rows % 16) // 16 + strips - 1
    early = min(chunk_rows // 16 + 2, strips)

    def strip_row(p):
        return pl.multiple_of(((first_strip + p) % strips) * 16, 16)

    def fetch(p):
        at = pl.ds(strip_row(p), 16)
        return pltpu.make_async_copy(level_ref.at[:, at, :], level_here.at[:, at, :], fetch_sem.at[p])

    rays = pltpu.make_async_copy(ray_ref, ray_here, ray_sem)
    for p in range(early):
        fetch(p).start()
    rays.start()
    for p in range(early, strips):
        fetch(p).start()

    def unpack(p):
        fetch(p).wait()
        r = strip_row(p)
        for k in range(slices):
            value = level_here[k, pl.ds(r, 16), :].astype(jnp.float32)
            at = pl.ds(pl.multiple_of(r + PAD, 8), 16)
            lev[k, at, LANES:LANES + cols] = value
            lev[k, at, 0:LANES] = jnp.broadcast_to(value[:, 0:1], (16, LANES))
            lev[k, at, LANES + cols:] = jnp.broadcast_to(value[:, cols - 1:cols], (16, LANES))

        @pl.when(r == 0)
        def _():
            for k in range(slices):
                lev[k, 0:PAD, :] = jnp.broadcast_to(
                    lev[k, PAD:PAD + 1, :], (PAD, cols + 2 * LANES))

        @pl.when(r == rows - 16)
        def _():
            for k in range(slices):
                lev[k, PAD + rows:, :] = jnp.broadcast_to(
                    lev[k, PAD + rows - 1:PAD + rows, :], (PAD, cols + 2 * LANES))

    period = slices * members
    base_phase = (2.0 * math.pi / period) * (first % period).astype(jnp.float32)
    band = []
    for c in range(3):
        angle = jnp.full((8, LANES), base_phase + 2.0 * math.pi / 3.0 * c, jnp.float32)
        band.append((0.5 * jnp.cos(angle), 0.5 * jnp.sin(angle)))
    first_real = first.astype(jnp.float32)

    def march(t):
        target = (group_id + 1 + t // subs) % groups
        sub = t % subs
        flat = part.at[t].reshape(5, members * block, LANES)

        @pl.loop(0, (chunk_rows // 8) * (chunk_cols // width))
        def _(i):
            local = (i // (chunk_cols // width)) * 8
            local_col = (i % (chunk_cols // width)) * width
            r0 = pl.multiple_of(target * chunk_rows + local, 8)
            c0 = pl.multiple_of(sub * chunk_cols + local_col, LANES)
            left_samples = ray_here[pl.ds(r0, 8), pl.ds(c0, width)] - first
            through = jnp.ones((8, width), jnp.float32)
            plain = jnp.zeros((8, width), jnp.float32)
            even = odd = distance = plain
            for k in range(slices):
                wide = lev[k, pl.ds(pl.multiple_of(r0 + PAD, 8), 8), pl.ds(c0, width + 2 * LANES)]
                total = width + 2 * LANES
                left = pltpu.roll(wide, 1, 1)[:, LANES:LANES + width]
                right = pltpu.roll(wide, total - 1, 1)[:, LANES:LANES + width]
                phi = wide[:, LANES:LANES + width]
                tall = lev[k, pl.ds(r0, 24), pl.ds(pl.multiple_of(c0 + LANES, LANES), width)]
                across = right - left
                downward = tall[9:17] - tall[7:15]
                facing = (0.48 * across + 0.6 * downward + 1.28) * lax.rsqrt(
                    across * across + downward * downward + 4.0)
                shading = 0.25 + 0.75 * jnp.maximum(facing, 0.0)
                opacity = jnp.exp2(phi * phi * (-4.0 / math.log(2.0)) + math.log2(9.0 / depths))
                opacity = jnp.where(left_samples > k, opacity, 0.0)
                weight = through * opacity
                through = through - weight
                distance = distance + weight * ((first_real + (k + 0.5)) / depths)
                shaded = weight * shading
                plain = plain + shaded
                even = even + shaded * math.cos(2.0 * math.pi * k / period)
                if k:
                    odd = odd + shaded * math.sin(2.0 * math.pi * k / period)
            for j in range(width // LANES):
                cut = slice(j * LANES, (j + 1) * LANES)
                at = pl.ds(local * tiles_wide + local_col // LANES + j, 8, stride=tiles_wide)
                for c in range(3):
                    flat[c, at, :] = (0.5 * plain[:, cut] + band[c][0] * even[:, cut]
                                      - band[c][1] * odd[:, cut])
                flat[3, at, :] = distance[:, cut]
                flat[4, at, :] = through[:, cut]

    def half(source, t, own):
        return source.at[t, :, :, own]

    def swap(bit, t):
        partner, own = flip_bit(member_id, bit)
        source = part if bit == 0 else arrive[bit - 1]
        return pltpu.make_async_remote_copy(
            src_ref=half(source, t, 1 - own), dst_ref=landing(bit, t),
            send_sem=send_sem.at[bit, t], recv_sem=recv_sem.at[bit, t],
            device_id=(group_id, partner), device_id_type=MESH)

    def landing(bit, t):
        held = arrive[bit].at[t]
        if bit < bits - 1:
            held = held.reshape(5, members >> (bit + 1), block, LANES)
        return held

    def hand_over(t):
        target = (group_id + 1 + t // subs) % groups
        return pltpu.make_async_remote_copy(
            src_ref=arrive[bits - 1].at[t], dst_ref=from_group.at[t],
            send_sem=gsend_sem.at[t], recv_sem=grecv_sem.at[t],
            device_id=(target, member_id), device_id_type=MESH)

    def blend(bit, t):
        _, own = flip_bit(member_id, bit)
        swap(bit, t).wait_recv()
        source = part if bit == 0 else arrive[bit - 1]
        mine_front = jnp.bitwise_and(jnp.right_shift(member_rank, bit), 1) == 0
        count = members >> (bit + 1)
        target = landing(bit, t)

        @pl.loop(0, count)
        def _(z):
            def kept(c):
                return source[t, c, z, own]

            def place(c):
                return (c, z) if bit < bits - 1 else (c, 0)
            mine, theirs = kept(4), target[place(4)]
            keep_scale = jnp.where(mine_front, 1.0, theirs)
            come_scale = jnp.where(mine_front, mine, 1.0)
            for c in range(4):
                target[place(c)] = keep_scale * kept(c) + come_scale * target[place(c)]
            target[place(4)] = mine * theirs

    pl.loop(0, early)(unpack)
    rays.wait()
    march(0)
    pl.semaphore_wait(barrier, bits + groups - 1)

    delay = [0] + [3 * b - 1 for b in range(1, bits)]

    @pl.loop(0, chunks + delay[-1])
    def _(t):
        @pl.when(t < chunks)
        def _():
            swap(0, t).start()

        @pl.when(t == subs - 1)
        def _():
            pl.loop(early, strips)(unpack)

        @pl.when(t < chunks - 1)
        def _():
            march(t + 1)
        for bit in range(bits):
            now = t - delay[bit]

            @pl.when((now >= 0) & (now < chunks))
            def _():
                blend(bit, now)
                if bit < bits - 1:
                    swap(bit + 1, now).start()
                else:
                    @pl.when(now < chunks - subs)
                    def _():
                        hand_over(now).start()

    @pl.loop(0, chunks - subs)
    def _(t):
        hand_over(t).wait_recv()

    def put(c, s, value):
        for q in range(block):
            at = (q // tiles_wide) * cols + (q % tiles_wide) * LANES + s * chunk_cols
            out_ref[c:c + 1, at:at + LANES] = value[q:q + 1, :]

    senders = [(group_id + 2 * groups - 1 - i) % groups for i in range(groups)]
    ranks = [jnp.bitwise_xor(s, group_mask) for s in senders]
    for s in range(subs):
        images = [from_group.at[i * subs + s] for i in range(groups - 1)]
        images.append(arrive[bits - 1].at[(groups - 1) * subs + s, :, 0])

        def piece(i, c):
            if i < groups - 1:
                return images[i][c, 0]
            return images[i][c]
        clear = [piece(i, 4) for i in range(groups)]
        total = [None] * 4
        for i in range(groups):
            ahead = None
            for h in range(groups):
                if h != i:
                    term = jnp.where(ranks[h] < ranks[i], clear[h], 1.0)
                    ahead = term if ahead is None else ahead * term
            for c in range(4):
                term = ahead * piece(i, c)
                total[c] = term if total[c] is None else total[c] + term
        for c in range(4):
            put(c, s, total[c])
        put(4, s, 1.0 - functools.reduce(lambda a, b: a * b, clear))

    @pl.loop(0, chunks)
    def _(t):
        for bit in range(bits):
            swap(bit, t).wait_send()

    @pl.loop(0, chunks - subs)
    def _(t):
        hand_over(t).wait_send()


def body(groups, members, level_set, ray_length, member_flip, group_flip):
    slices, rows, cols = level_set.shape
    bits = members.bit_length() - 1
    pixels = rows * cols // (groups * members)
    whole_rows = pixels % cols == 0
    subs = 1
    while whole_rows and subs < 4 and pixels % (2 * subs * 8 * LANES) == 0:
        subs *= 2
    block = pixels // LANES // subs
    chunks = groups * subs
    cfg = (groups, members, bits, slices, rows, cols, subs, block)
    arrive = []
    for bit in range(bits):
        count = members >> (bit + 1)
        shape = (count // 2, 2) if bit < bits - 1 else (1,)
        arrive.append(pltpu.VMEM((chunks, 5) + shape + (block, LANES), jnp.float32))
    vmem = pl.BlockSpec(memory_space=pltpu.VMEM)
    anywhere = pl.BlockSpec(memory_space=pl.ANY)
    smem = pl.BlockSpec(memory_space=pltpu.SMEM)
    return pl.pallas_call(
        functools.partial(kernel, cfg),
        out_shape=jax.ShapeDtypeStruct((5, pixels), jnp.float32),
        in_specs=[anywhere, anywhere, smem, smem],
        out_specs=vmem,
        scratch_shapes=[
            pltpu.VMEM((slices, rows, cols), level_set.dtype),
            pltpu.VMEM((rows, cols), ray_length.dtype),
            pltpu.SemaphoreType.DMA((rows // 16,)),
            pltpu.SemaphoreType.DMA,
            pltpu.VMEM((slices, rows + 2 * PAD, cols + 2 * LANES), jnp.float32),
            pltpu.VMEM((chunks, 5, members // 2, 2, block, LANES), jnp.float32),
            *arrive,
            pltpu.VMEM((chunks - subs, 5, 1, block, LANES), jnp.float32),
            pltpu.SemaphoreType.DMA((bits, chunks)),
            pltpu.SemaphoreType.DMA((bits, chunks)),
            pltpu.SemaphoreType.DMA((chunks - subs,)),
            pltpu.SemaphoreType.DMA((chunks - subs,)),
        ],
        compiler_params=pltpu.CompilerParams(
            collective_id=0, has_side_effects=True, vmem_limit_bytes=60 * 1024 * 1024),
        cost_estimate=pl.CostEstimate(
            flops=40 * slices * rows * cols, bytes_accessed=level_set.size * 2,
            transcendentals=2 * slices * rows * cols),
    )(level_set, ray_length, member_flip, group_flip)


def solution(mesh):
    in_specs = (P(("group", "member"), None, None), P(), P("group"), P())
    out_specs = P(None, ("group", "member"))
    run = functools.partial(body, mesh.shape["group"], mesh.shape["member"])
    return jax.shard_map(run, mesh=mesh, in_specs=in_specs, out_specs=out_specs, check_vma=False)
```
